32 devices in a mesh: section: 2 (over y), fsdp: 16 (over z, x, core).
Axes of the slice: x: 2, y: 2, z: 4, core: 2. Of those that a mesh axis runs over, the one named last changes fastest.
Arguments:
- ends: bfloat16 [2, 2, 16, 256, 768], P('section', None, 'fsdp'), may hold values from -6 to 6
- lengths: int32 [2, 16], P(None, 'fsdp'), may hold values from 1 to 256, 2560 in all within a row
- w_qkv: bfloat16 [2, 768, 2304], P('section', 'fsdp'), as said below
- w_out: bfloat16 [2, 768, 768], P('section', 'fsdp'), may hold values from -0.4375 to 0.4375
- w_up: bfloat16 [2, 768, 3072], P('section', 'fsdp'), may hold values from -0.21875 to 0.21875
- w_down: bfloat16 [2, 3072, 768], P('section', 'fsdp'), may hold values from -0.109375 to 0.109375
- vectors: bfloat16 [2, 9216], P('section', 'fsdp'), as said below
Outputs:
- ends_out: float32 [2, 2, 16, 256, 768], P('section', None, 'fsdp')
- grad_w_qkv: float32 [2, 768, 2304], P('section', 'fsdp')
- grad_w_out: float32 [2, 768, 768], P('section', 'fsdp')
- grad_w_up: float32 [2, 768, 3072], P('section', 'fsdp')
- grad_w_down: float32 [2, 3072, 768], P('section', 'fsdp')
- grad_vectors: float32 [2, 9216], P('section', 'fsdp')
The draws below stay inside these ranges and needn't reach their ends.
Inputs may be any that keep to these rules, and one draw needn't show every extreme that they name: Sequence s of micro-batch m is its first lengths[m, s] positions, the rest is padding; in each micro-batch the 16 lengths sum to 2560 and the longest is 256. `w_qkv`: columns 0 to 767 are the query projection, 768 to 1535 the key projection, the rest the value projection. `vectors`: laid out as in the reference program: bq, bv, bo, g1, s1, bu, bd, g2, s2.
All inputs are finite; a program needn't handle non-finite values. No bound on the sum of `lengths` on one device may be relied on, other than what follows from the above.
Results may differ from the reference program's by a relative error of at most 0.014.
Values may be sent and summed in bfloat16 or wider, within the bound.
A program may use at most 192 MiB of HBM per device.

```python
import math
import jax
import jax.numpy as jnp
import numpy as np
from jax import lax

D = 768
HEADS = 12
FF = 3072
HEAD = 64
L = 256
MICRO = 2
SEQS = 16
VEC = 9216


def draw_w_qkv(key, part):
    base_key = jax.random.fold_in(jax.random.fold_in(key, 11), 0)
    return (jnp.clip(jax.random.normal(base_key, (2, D, 3 * D), jnp.float32), -5.0, 5.0) / math.sqrt(D)).astype(jnp.bfloat16)


def draw_vectors(key, part):
    gain_key, bias_key = jax.random.split(jax.random.fold_in(key, 23))
    position = jnp.arange(8 * D + FF)
    is_gain = (position >= 3 * D) & (position < 4 * D) | (position >= 6 * D + FF) & (position < 7 * D + FF)
    gains = jax.random.uniform(gain_key, (2, VEC), jnp.float32, 0.5, 1.5)
    biases = 0.5 * jnp.clip(jax.random.normal(bias_key, (2, VEC), jnp.float32), -2.5, 2.5)
    return jnp.where(is_gain[None, :], gains, biases).astype(jnp.bfloat16)


def strengthened(array, own_key, source, target, shards_of, factor):
    def block_of(axis_at):
        return (jnp.arange(array.shape[axis_at]) // (array.shape[axis_at] // shards_of)).reshape((-1,) + (1,) * (array.ndim - 1 - axis_at))

    one_side = jax.random.permutation(own_key, shards_of)[block_of(target)]
    other_side = (block_of(target) + shards_of // 2) % shards_of
    return jnp.where((block_of(source) == one_side) | (block_of(source) == other_side), factor * array, array)


def block_scale(stream_key, dims, cuts, least, top_value):
    def one(axis_at, shards_of):
        heights = jax.random.uniform(jax.random.fold_in(jax.random.fold_in(stream_key, 6), axis_at), (shards_of,), jnp.float32, least / len(cuts), top_value / len(cuts))
        return jnp.repeat(jnp.exp(heights), dims[axis_at] // shards_of).reshape((-1,) + (1,) * (len(dims) - axis_at - 1))

    gain = one(*cuts[0])
    for cut in cuts[1:]:
        gain = gain * one(*cut)
    return gain


def profile(number_of, total, reach, lean):
    loads = [(1 << 20) // math.isqrt(grade ** lean) + 1 for grade in range(2, number_of + 1)]
    spare, counts = total - reach - (number_of - 1), [1] * (number_of - 1)
    while spare > 0:
        movable = [i for i in range(number_of - 1) if counts[i] < reach]
        mass, budget = sum([loads[i] for i in movable]), spare
        for i in movable:
            extra = min(reach - counts[i], max(1, budget * loads[i] // mass), spare)
            counts[i] = counts[i] + extra
            spare = spare - extra
    return np.array([reach] + counts)


def uneven(own_key, number_of, total, most, lean):
    if number_of == 2:
        one = jax.random.randint(own_key, (), max(1, total - most), min(most, total - 1) + 1)
        return jnp.stack([one, total - one])
    tallies = jnp.asarray(profile(number_of, total, most, lean), jnp.int32)
    twos = (number_of - 1) // 2
    donor, receiver = tallies[1:1 + 2 * twos:2], tallies[2:2 + 2 * twos:2]
    margin = jnp.minimum(donor - 1, most - receiver)
    passed = jax.random.randint(jax.random.fold_in(own_key, 1), (twos,), 0, 1 << 20) % (margin + 1)
    tallies = tallies.at[1:1 + 2 * twos:2].set(donor - passed).at[2:2 + 2 * twos:2].set(receiver + passed)
    return tallies[jax.random.permutation(jax.random.fold_in(own_key, 2), number_of)]


def gaussian(own_key, extent, scale, reach, cuts=(), held_as=jnp.bfloat16):
    gain = block_scale(own_key, extent, cuts, -0.22, 0.18) if cuts else 1.0
    drawn = jax.random.normal(own_key, extent, jnp.float32) * scale * gain
    return jnp.minimum(jnp.maximum(drawn, -reach), reach).astype(held_as)


def gaussian_with(key, shape, deviation, bound, cuts, heavy, kind=jnp.bfloat16):
    array = deviation * jax.random.normal(key, shape, jnp.float32)
    if cuts:
        array = array * block_scale(key, shape, cuts, -0.22, 0.18)
    return jnp.clip(strengthened(array, jax.random.fold_in(key, 3), *heavy), -bound, bound).astype(kind)


def setup_inputs(seed: int = 0) -> dict:
    streams_of = jax.random.split(jax.random.key(seed), 8)
    return {
        "ends": gaussian_with(streams_of[0], (2, MICRO, SEQS, L, D), 1.0, 6.0, ((0, 2), (2, 16)), (2, 4, 16, 2.0)),
        "lengths": jax.vmap(lambda own: uneven(own, SEQS, SEQS * L * 5 // 8, L, 2))(jax.random.split(streams_of[1], MICRO)).reshape((MICRO, SEQS)).astype(jnp.int32),
        "w_qkv": draw_w_qkv(jax.random.fold_in(streams_of[7], 71), 0),
        "w_out": gaussian(streams_of[3], (2, D, D), (D * 64 // L) ** -0.5, 0.4375, ((0, 2), (1, 16))),
        "w_up": gaussian(streams_of[4], (2, D, FF), D ** -0.5, 0.21875, ((0, 2), (1, 16))),
        "w_down": gaussian(streams_of[5], (2, FF, D), FF ** -0.5, 0.109375, ((0, 2), (1, 16))),
        "vectors": draw_vectors(jax.random.fold_in(streams_of[7], 71), 0),
    }


def split_vector(vec):
    flat_vec = vec.astype(jnp.float32)
    widths = [D, D, D, D, D, FF, D, D, D]
    pieces = []
    offset = 0
    for width in widths:
        pieces.append(flat_vec[offset:offset + width])
        offset = offset + width
    return tuple(pieces)

def normalize(hidden):
    mean_row = lax.optimization_barrier(jnp.mean(hidden, axis=-1, keepdims=True))
    centred = hidden - mean_row
    variance = lax.optimization_barrier(jnp.mean(centred * centred, axis=-1, keepdims=True))
    inv_std = lax.rsqrt(variance + 1e-12)
    return (centred * inv_std, inv_std)

def norm_back(grad_n, normed, inv_std):
    return inv_std * (grad_n - lax.optimization_barrier(jnp.mean(grad_n, axis=-1, keepdims=True)) - normed * lax.optimization_barrier(jnp.mean(grad_n * normed, axis=-1, keepdims=True)))

def gelu_value(up_in):
    return 0.5 * up_in * (1.0 + lax.erf(up_in * 0.7071067811865476))

def gelu_slope(up_in):
    return 0.5 * (1.0 + lax.erf(up_in * 0.7071067811865476)) + up_in * jnp.exp(-0.5 * up_in * up_in) * 0.3989422804014327

def heads_of(matrix):
    return matrix.astype(jnp.float32).reshape(matrix.shape[0], HEADS, HEAD)

def scores_of(query_b, key_b, visible):
    scores = jnp.einsum('qhd,khd->hqk', heads_of(query_b), heads_of(key_b)) * HEAD ** (-0.5)
    return jnp.where(visible[None, None, :], scores, -1e+30)

def attend(query_b, key_b, value_b, visible):
    row_count = query_b.shape[0]
    masked = scores_of(query_b, key_b, visible)
    row_peak = lax.optimization_barrier(jnp.max(masked, axis=-1, keepdims=True))
    log_total = row_peak + jnp.log(lax.optimization_barrier(jnp.sum(jnp.exp(masked - row_peak), axis=-1, keepdims=True)))
    attn_probs = jnp.where(visible[None, None, :], jnp.exp(masked - log_total), 0.0)
    probs_b = attn_probs.astype(jnp.bfloat16)
    context = jnp.einsum('hqk,khd->qhd', probs_b.astype(jnp.float32), heads_of(value_b))
    return (log_total, context.reshape(row_count, D))

def attend_back(grad_ctx_b, query_b, key_b, value_b, log_total, context, visible):
    row_count = query_b.shape[0]
    masked = scores_of(query_b, key_b, visible)
    attn_probs = jnp.where(visible[None, None, :], jnp.exp(masked - log_total), 0.0)
    probs_b = attn_probs.astype(jnp.bfloat16)
    grad_heads = heads_of(grad_ctx_b)
    grad_v = jnp.einsum('hqk,qhd->khd', probs_b.astype(jnp.float32), grad_heads)
    grad_p = jnp.einsum('qhd,khd->hqk', grad_heads, heads_of(value_b))
    delta_rows = lax.optimization_barrier(jnp.sum(grad_heads * context.reshape(row_count, HEADS, HEAD), axis=-1))
    grad_s = attn_probs * (grad_p - jnp.transpose(delta_rows)[:, :, None]) * HEAD ** (-0.5)
    grad_s_b = grad_s.astype(jnp.bfloat16).astype(jnp.float32)
    grad_q = jnp.einsum('hqk,khd->qhd', grad_s_b, heads_of(key_b))
    grad_k = jnp.einsum('hqk,qhd->khd', grad_s_b, heads_of(query_b))
    return jnp.concatenate([grad_q.reshape(row_count, D), grad_k.reshape(row_count, D), grad_v.reshape(row_count, D)], axis=1)

def layer_forward(x_in, visible, params):
    w_qkv, w_out, w_up, w_down, vec = params
    bias_q, bias_v, bias_o, gain1, shift1, bias_up, bias_down, gain2, shift2 = split_vector(vec)
    projected = jnp.dot(x_in, w_qkv, preferred_element_type=jnp.float32)
    query_b = (projected[:, :D] + bias_q).astype(jnp.bfloat16)
    key_b = projected[:, D:2 * D].astype(jnp.bfloat16)
    value_b = (projected[:, 2 * D:] + bias_v).astype(jnp.bfloat16)
    log_total, context = attend(query_b, key_b, value_b, visible)
    pre_one = x_in.astype(jnp.float32) + jnp.dot(context.astype(jnp.bfloat16), w_out, preferred_element_type=jnp.float32) + bias_o
    normed1, inv_std1 = normalize(pre_one)
    hidden1 = normed1 * gain1 + shift1
    hidden1_b = hidden1.astype(jnp.bfloat16)
    up_pre = jnp.dot(hidden1_b, w_up, preferred_element_type=jnp.float32) + bias_up
    act_b = gelu_value(up_pre).astype(jnp.bfloat16)
    pre_two = hidden1 + jnp.dot(act_b, w_down, preferred_element_type=jnp.float32) + bias_down
    normed2, inv_std2 = normalize(pre_two)
    result = normed2 * gain2 + shift2
    kept_state = (x_in, query_b, key_b, value_b, log_total, context, normed1, inv_std1, hidden1_b, up_pre, act_b, normed2, inv_std2)
    return (result, kept_state)

def layer_backward(d_out, kept_state, visible, params):
    w_qkv, w_out, w_up, w_down, vec = params
    bias_q, bias_v, bias_o, gain1, shift1, bias_up, bias_down, gain2, shift2 = split_vector(vec)
    x_in, query_b, key_b, value_b, log_total, context, normed1, inv_std1, hidden1_b, up_pre, act_b, normed2, inv_std2 = kept_state
    grad_gain2 = lax.optimization_barrier(jnp.sum(d_out * normed2, axis=0))
    grad_shift2 = lax.optimization_barrier(jnp.sum(d_out, axis=0))
    grad_pre2 = norm_back(d_out * gain2, normed2, inv_std2)
    grad_pre2_b = grad_pre2.astype(jnp.bfloat16)
    grad_bdown = lax.optimization_barrier(jnp.sum(grad_pre2, axis=0))
    grad_wdown = jnp.dot(act_b.T, grad_pre2_b, preferred_element_type=jnp.float32)
    grad_up = jnp.dot(grad_pre2_b, w_down.T, preferred_element_type=jnp.float32) * gelu_slope(up_pre)
    grad_up_b = grad_up.astype(jnp.bfloat16)
    grad_bup = lax.optimization_barrier(jnp.sum(grad_up, axis=0))
    grad_wup = jnp.dot(hidden1_b.T, grad_up_b, preferred_element_type=jnp.float32)
    grad_h1 = grad_pre2 + jnp.dot(grad_up_b, w_up.T, preferred_element_type=jnp.float32)
    grad_gain1 = lax.optimization_barrier(jnp.sum(grad_h1 * normed1, axis=0))
    grad_shift1 = lax.optimization_barrier(jnp.sum(grad_h1, axis=0))
    grad_pre1 = norm_back(grad_h1 * gain1, normed1, inv_std1)
    grad_pre1_b = grad_pre1.astype(jnp.bfloat16)
    grad_bout = lax.optimization_barrier(jnp.sum(grad_pre1, axis=0))
    grad_wout = jnp.dot(context.astype(jnp.bfloat16).T, grad_pre1_b, preferred_element_type=jnp.float32)
    grad_ctx_b = jnp.dot(grad_pre1_b, w_out.T, preferred_element_type=jnp.float32).astype(jnp.bfloat16)
    grad_proj = attend_back(grad_ctx_b, query_b, key_b, value_b, log_total, context, visible)
    grad_proj_b = grad_proj.astype(jnp.bfloat16)
    grad_bq = lax.optimization_barrier(jnp.sum(grad_proj[:, :D], axis=0))
    grad_bv = lax.optimization_barrier(jnp.sum(grad_proj[:, 2 * D:], axis=0))
    grad_wqkv = jnp.dot(x_in.T, grad_proj_b, preferred_element_type=jnp.float32)
    grad_x = grad_pre1 + jnp.dot(grad_proj_b, w_qkv.T, preferred_element_type=jnp.float32)
    grad_vec = jnp.concatenate([grad_bq, grad_bv, grad_bout, grad_gain1, grad_shift1, grad_bup, grad_bdown, grad_gain2, grad_shift2])
    return (grad_x, (grad_wqkv, grad_wout, grad_wup, grad_wdown, grad_vec))

def reference(ends, lengths, w_qkv, w_out, w_up, w_down, vectors):
    inputs = ends[0].reshape(MICRO * SEQS, L, D)
    cotangents = ends[1].reshape(MICRO * SEQS, L, D)
    seq_lengths = lengths.reshape(MICRO * SEQS).astype(jnp.int32)
    params0 = (w_qkv[0], w_out[0], w_up[0], w_down[0], vectors[0])
    params1 = (w_qkv[1], w_out[1], w_up[1], w_down[1], vectors[1])
    zeros0 = tuple((jnp.zeros(w.shape, jnp.float32) for w in params0))
    zeros1 = tuple((jnp.zeros(w.shape, jnp.float32) for w in params1))
    positions = jnp.arange(L, dtype=jnp.int32)

    def one_sequence(carry, item):
        grads0, grads1 = carry
        x_in, cotangent, length = item
        visible = positions < length
        result0, kept0 = layer_forward(x_in, visible, params0)
        result1, kept1 = layer_forward(result0.astype(jnp.bfloat16), visible, params1)
        d_out1 = cotangent.astype(jnp.float32) * visible[:, None].astype(jnp.float32)
        grad_x1, terms1 = layer_backward(d_out1, kept1, visible, params1)
        grad_z = lax.optimization_barrier(grad_x1.astype(jnp.bfloat16)).astype(jnp.float32)
        grad_x0, terms0 = layer_backward(grad_z, kept0, visible, params0)
        grads0 = jax.tree.map(lambda total, term: total + term, grads0, terms0)
        grads1 = jax.tree.map(lambda total, term: total + term, grads1, terms1)
        return ((grads0, grads1), (grad_x0, result1))
    (grads0, grads1), (grad_inputs, outputs) = lax.scan(one_sequence, (zeros0, zeros1), (inputs, cotangents, seq_lengths))
    ends_out = jnp.stack([grad_inputs.reshape(MICRO, SEQS, L, D), outputs.reshape(MICRO, SEQS, L, D)])
    stacked = [jnp.stack([first_g, second_g]) for first_g, second_g in zip(grads0, grads1)]
    return (ends_out, stacked[0], stacked[1], stacked[2], stacked[3], stacked[4])
```

```python
import jax
import jax.numpy as jnp
from jax import lax
from jax.sharding import PartitionSpec as P

D = 768
HEADS = 12
FF = 3072
HEAD = 64


def shifted(value, axis, steps):
    count = lax.axis_size(axis)
    first, last = (max(0, -steps), min(count, count - steps))
    return lax.ppermute(value, axis, [(source, source + steps) for source in range(first, last)])


def split_vector(vec):
    flat_vec = vec.astype(jnp.float32)
    widths = [D, D, D, D, D, FF, D, D, D]
    pieces = []
    offset = 0
    for width in widths:
        pieces.append(flat_vec[offset : offset + width])
        offset = offset + width
    return tuple(pieces)


def normalize(hidden):
    mean_row = jnp.mean(hidden, axis=-1, keepdims=True)
    centred = hidden - mean_row
    variance = jnp.mean(centred * centred, axis=-1, keepdims=True)
    inv_std = lax.rsqrt(variance + 1e-12)
    return (centred * inv_std, inv_std)


def norm_back(grad_n, normed, inv_std):
    return inv_std * (
        grad_n
        - jnp.mean(grad_n, axis=-1, keepdims=True)
        - normed * jnp.mean(grad_n * normed, axis=-1, keepdims=True)
    )


def gelu_value(up_in):
    return 0.5 * up_in * (1.0 + lax.erf(up_in * 0.7071067811865476))


def gelu_slope(up_in):
    return (
        0.5 * (1.0 + lax.erf(up_in * 0.7071067811865476))
        + up_in * jnp.exp(-0.5 * up_in * up_in) * 0.3989422804014327
    )


def left_dot(left, right):
    return lax.dot_general(
        left, right, (((0,), (0,)), ((), ())), preferred_element_type=jnp.float32
    )


def right_dot(left, right):
    return lax.dot_general(
        left, right, (((1,), (1,)), ((), ())), preferred_element_type=jnp.float32
    )


def rows_of(value, groups):
    return value.reshape(groups, value.shape[0] // groups, HEADS, HEAD)


def scores_of(query_b, key_b, visible):
    groups = visible.shape[0]
    scores = jnp.einsum(
        "bqhd,bkhd->bhqk",
        rows_of(query_b, groups),
        rows_of(key_b, groups),
        preferred_element_type=jnp.float32,
    ) * HEAD ** (-0.5)
    return jnp.where(visible[:, None, None, :], scores, -1e30)


def attend(query_b, key_b, value_b, visible):
    groups = visible.shape[0]
    masked = scores_of(query_b, key_b, visible)
    row_peak = jnp.max(masked, axis=-1, keepdims=True)
    log_total = row_peak + jnp.log(jnp.sum(jnp.exp(masked - row_peak), axis=-1, keepdims=True))
    probs_b = jnp.exp(masked - log_total).astype(jnp.bfloat16)
    context = jnp.einsum(
        "bhqk,bkhd->bqhd", probs_b, rows_of(value_b, groups), preferred_element_type=jnp.float32
    )
    return (log_total, context.reshape(-1, D))


def attend_back(grad_ctx_b, query_b, key_b, value_b, log_total, context, visible):
    groups = visible.shape[0]
    masked = scores_of(query_b, key_b, visible)
    attn_probs = jnp.exp(masked - log_total)
    probs_b = attn_probs.astype(jnp.bfloat16)
    grad_heads = rows_of(grad_ctx_b, groups)
    grad_v = jnp.einsum("bhqk,bqhd->bkhd", probs_b, grad_heads, preferred_element_type=jnp.float32)
    grad_p = jnp.einsum(
        "bqhd,bkhd->bhqk", grad_heads, rows_of(value_b, groups), preferred_element_type=jnp.float32
    )
    delta_rows = jnp.sum(grad_heads.astype(jnp.float32) * rows_of(context, groups), axis=-1)
    grad_s = attn_probs * (grad_p - jnp.swapaxes(delta_rows, 1, 2)[..., None]) * HEAD ** (-0.5)
    grad_s_b = grad_s.astype(jnp.bfloat16)
    grad_q = jnp.einsum(
        "bhqk,bkhd->bqhd", grad_s_b, rows_of(key_b, groups), preferred_element_type=jnp.float32
    )
    grad_k = jnp.einsum(
        "bhqk,bqhd->bkhd", grad_s_b, rows_of(query_b, groups), preferred_element_type=jnp.float32
    )
    return jnp.concatenate(
        [grad_q.reshape(-1, D), grad_k.reshape(-1, D), grad_v.reshape(-1, D)], axis=1
    )


def layer_forward(x_in, visible, params):
    w_qkv, w_out, w_up, w_down, vec = params
    bias_q, bias_v, bias_o, gain1, shift1, bias_up, bias_down, gain2, shift2 = split_vector(vec)
    projected = jnp.dot(x_in, w_qkv, preferred_element_type=jnp.float32)
    query_b = (projected[:, :D] + bias_q).astype(jnp.bfloat16)
    key_b = projected[:, D : 2 * D].astype(jnp.bfloat16)
    value_b = (projected[:, 2 * D :] + bias_v).astype(jnp.bfloat16)
    log_total, context = attend(query_b, key_b, value_b, visible)
    pre_one = (
        x_in.astype(jnp.float32)
        + jnp.dot(context.astype(jnp.bfloat16), w_out, preferred_element_type=jnp.float32)
        + bias_o
    )
    normed1, inv_std1 = normalize(pre_one)
    hidden1 = normed1 * gain1 + shift1
    hidden1_b = hidden1.astype(jnp.bfloat16)
    up_pre = jnp.dot(hidden1_b, w_up, preferred_element_type=jnp.float32) + bias_up
    act_b = gelu_value(up_pre).astype(jnp.bfloat16)
    pre_two = hidden1 + jnp.dot(act_b, w_down, preferred_element_type=jnp.float32) + bias_down
    normed2, inv_std2 = normalize(pre_two)
    result = normed2 * gain2 + shift2
    kept_state = (
        x_in,
        query_b,
        key_b,
        value_b,
        log_total,
        context,
        normed1,
        inv_std1,
        hidden1_b,
        up_pre,
        act_b,
        normed2,
        inv_std2,
    )
    return (result, kept_state)


def layer_backward(d_out, kept_state, visible, params):
    w_qkv, w_out, w_up, w_down, vec = params
    bias_q, bias_v, bias_o, gain1, shift1, bias_up, bias_down, gain2, shift2 = split_vector(vec)
    (
        x_in,
        query_b,
        key_b,
        value_b,
        log_total,
        context,
        normed1,
        inv_std1,
        hidden1_b,
        up_pre,
        act_b,
        normed2,
        inv_std2,
    ) = kept_state
    grad_gain2 = jnp.sum(d_out * normed2, axis=0)
    grad_shift2 = jnp.sum(d_out, axis=0)
    grad_pre2 = norm_back(d_out * gain2, normed2, inv_std2)
    grad_pre2_b = grad_pre2.astype(jnp.bfloat16)
    grad_bdown = jnp.sum(grad_pre2, axis=0)
    grad_up = right_dot(grad_pre2_b, w_down) * gelu_slope(up_pre)
    grad_up_b = grad_up.astype(jnp.bfloat16)
    grad_bup = jnp.sum(grad_up, axis=0)
    grad_h1 = grad_pre2 + right_dot(grad_up_b, w_up)
    grad_gain1 = jnp.sum(grad_h1 * normed1, axis=0)
    grad_shift1 = jnp.sum(grad_h1, axis=0)
    grad_pre1 = norm_back(grad_h1 * gain1, normed1, inv_std1)
    grad_pre1_b = grad_pre1.astype(jnp.bfloat16)
    grad_bout = jnp.sum(grad_pre1, axis=0)
    context_b = context.astype(jnp.bfloat16)
    grad_ctx_b = right_dot(grad_pre1_b, w_out).astype(jnp.bfloat16)
    grad_proj = attend_back(grad_ctx_b, query_b, key_b, value_b, log_total, context, visible)
    grad_proj_b = grad_proj.astype(jnp.bfloat16)
    grad_bq = jnp.sum(grad_proj[:, :D], axis=0)
    grad_bv = jnp.sum(grad_proj[:, 2 * D :], axis=0)
    grad_x = grad_pre1 + right_dot(grad_proj_b, w_qkv)
    grad_vec = jnp.concatenate(
        [
            grad_bq,
            grad_bv,
            grad_bout,
            grad_gain1,
            grad_shift1,
            grad_bup,
            grad_bdown,
            grad_gain2,
            grad_shift2,
        ]
    )
    operands = (
        (x_in, grad_proj_b),
        (context_b, grad_pre1_b),
        (hidden1_b, grad_up_b),
        (act_b, grad_pre2_b),
    )
    return (grad_x, grad_vec, operands)


def gather_params(shards):
    return tuple(lax.all_gather(shard, "fsdp", axis=0, tiled=True) for shard in shards)


def gather_with_vector(w_shard, vec_shard):
    count = lax.axis_size("fsdp")
    rows, width = w_shard.shape
    padded = jnp.pad(vec_shard[None, :], ((0, 15), (0, width - vec_shard.shape[0])))
    joined = lax.all_gather(jnp.concatenate([w_shard, padded], axis=0), "fsdp", axis=0)
    weight = joined[:, :rows].reshape(count * rows, width)
    return weight, joined[:, rows, : vec_shard.shape[0]].reshape(-1)


def scatter_sum(value):
    total = lax.psum_scatter(
        value.astype(jnp.bfloat16), "fsdp", scatter_dimension=0, tiled=True
    )
    return total.astype(jnp.float32)


def scatter_with_vector(w_grad, vec_grad):
    count = lax.axis_size("fsdp")
    width = w_grad.shape[1]
    rows = w_grad.shape[0] // count
    share = vec_grad.shape[0] // count
    padded = jnp.pad(vec_grad.reshape(count, 1, share), ((0, 0), (0, 15), (0, width - share)))
    joined = jnp.concatenate([w_grad.reshape(count, rows, width), padded], axis=1)
    total = scatter_sum(joined.reshape(-1, width))
    return total[:rows], total[rows, :share]


def body(ends, lengths, w_qkv, w_out, w_up, w_down, vectors):
    is_first = lax.axis_index("section") == 0
    micro, row_count = ends.shape[1], ends.shape[3]
    local_rows = ends[0, :, 0].reshape(micro * row_count, D)
    positions = jnp.arange(row_count, dtype=jnp.int32)
    visible = positions[None, :] < lengths[:, 0][:, None]
    full_out, full_vec = gather_with_vector(w_out[0], vectors[0])
    full_qkv, full_up, full_down = gather_params((w_qkv[0], w_up[0], w_down[0]))
    params = (full_qkv, full_out, full_up, full_down, full_vec)
    early, _ = layer_forward(local_rows, visible, params)
    received = shifted(early.astype(jnp.bfloat16), "section", 1)
    x_in = jnp.where(is_first, local_rows, received)
    result, kept_state = layer_forward(x_in, visible, params)
    row_mask = visible.reshape(-1, 1).astype(jnp.float32)
    cotangent = local_rows.astype(jnp.float32) * row_mask
    early_grad, _, _ = layer_backward(cotangent, kept_state, visible, params)
    back_received = shifted(early_grad.astype(jnp.bfloat16), "section", -1)
    d_out = jnp.where(is_first, back_received.astype(jnp.float32), cotangent)
    grad_x, grad_vec, operands = layer_backward(d_out, kept_state, visible, params)
    grad_down = scatter_sum(left_dot(*operands[3]))
    grad_up = scatter_sum(left_dot(*operands[2]))
    grad_qkv = scatter_sum(left_dot(*operands[0]))
    grad_out, grad_vectors = scatter_with_vector(left_dot(*operands[1]), grad_vec)
    ends_out = jnp.where(is_first, grad_x, result).reshape(1, micro, 1, row_count, D)
    return (
        ends_out,
        grad_qkv[None],
        grad_out[None],
        grad_up[None],
        grad_down[None],
        grad_vectors[None],
    )


def solution(mesh):
    in_specs = (
        P("section", None, "fsdp", None, None),
        P(None, "fsdp"),
        P("section", "fsdp", None),
        P("section", "fsdp", None),
        P("section", "fsdp", None),
        P("section", "fsdp", None),
        P("section", "fsdp"),
    )
    out_specs = (
        P("section", None, "fsdp", None, None),
        P("section", "fsdp", None),
        P("section", "fsdp", None),
        P("section", "fsdp", None),
        P("section", "fsdp", None),
        P("section", "fsdp"),
    )
    return jax.shard_map(body, mesh=mesh, in_specs=in_specs, out_specs=out_specs, check_vma=False)
```

```python
import jax
import jax.numpy as jnp
from jax import lax
from jax.sharding import PartitionSpec as P

D = 768
HEADS = 12
FF = 3072
HEAD = 64


def shifted(value, axis, steps):
    count = lax.axis_size(axis)
    first, last = (max(0, -steps), min(count, count - steps))
    return lax.ppermute(value, axis, [(source, source + steps) for source in range(first, last)])


def split_vector(vec):
    flat_vec = vec.astype(jnp.float32)
    widths = [D, D, D, D, D, FF, D, D, D]
    pieces = []
    offset = 0
    for width in widths:
        pieces.append(flat_vec[offset : offset + width])
        offset = offset + width
    return tuple(pieces)


def normalize(hidden):
    mean_row = jnp.mean(hidden, axis=-1, keepdims=True)
    centred = hidden - mean_row
    variance = jnp.mean(centred * centred, axis=-1, keepdims=True)
    inv_std = lax.rsqrt(variance + 1e-12)
    return (centred * inv_std, inv_std)


def norm_back(grad_n, normed, inv_std):
    return inv_std * (
        grad_n
        - jnp.mean(grad_n, axis=-1, keepdims=True)
        - normed * jnp.mean(grad_n * normed, axis=-1, keepdims=True)
    )


def gelu_value(up_in):
    return 0.5 * up_in * (1.0 + lax.erf(up_in * 0.7071067811865476))


def gelu_slope(up_in):
    return (
        0.5 * (1.0 + lax.erf(up_in * 0.7071067811865476))
        + up_in * jnp.exp(-0.5 * up_in * up_in) * 0.3989422804014327
    )


def left_dot(left, right):
    return lax.dot_general(
        left, right, (((0,), (0,)), ((), ())), preferred_element_type=jnp.float32
    )


def right_dot(left, right):
    return lax.dot_general(
        left, right, (((1,), (1,)), ((), ())), preferred_element_type=jnp.float32
    )


def rows_of(value, groups):
    return value.reshape(groups, value.shape[0] // groups, HEADS, HEAD)


def scores_of(query_b, key_b, visible):
    groups = visible.shape[0]
    scores = jnp.einsum(
        "bqhd,bkhd->bhqk",
        rows_of(query_b, groups),
        rows_of(key_b, groups),
        preferred_element_type=jnp.float32,
    ) * HEAD ** (-0.5)
    return jnp.where(visible[:, None, None, :], scores, -1e30)


def attend(query_b, key_b, value_b, visible):
    groups = visible.shape[0]
    masked = scores_of(query_b, key_b, visible)
    row_peak = jnp.max(masked, axis=-1, keepdims=True)
    log_total = row_peak + jnp.log(jnp.sum(jnp.exp(masked - row_peak), axis=-1, keepdims=True))
    probs_b = jnp.exp(masked - log_total).astype(jnp.bfloat16)
    context = jnp.einsum(
        "bhqk,bkhd->bqhd", probs_b, rows_of(value_b, groups), preferred_element_type=jnp.float32
    )
    return (log_total, context.reshape(-1, D))


def attend_back(grad_ctx_b, query_b, key_b, value_b, log_total, context, visible):
    groups = visible.shape[0]
    masked = scores_of(query_b, key_b, visible)
    attn_probs = jnp.exp(masked - log_total)
    probs_b = attn_probs.astype(jnp.bfloat16)
    grad_heads = rows_of(grad_ctx_b, groups)
    grad_v = jnp.einsum("bhqk,bqhd->bkhd", probs_b, grad_heads, preferred_element_type=jnp.float32)
    grad_p = jnp.einsum(
        "bqhd,bkhd->bhqk", grad_heads, rows_of(value_b, groups), preferred_element_type=jnp.float32
    )
    delta_rows = jnp.sum(grad_heads.astype(jnp.float32) * rows_of(context, groups), axis=-1)
    grad_s = attn_probs * (grad_p - jnp.swapaxes(delta_rows, 1, 2)[..., None]) * HEAD ** (-0.5)
    grad_s_b = grad_s.astype(jnp.bfloat16)
    grad_q = jnp.einsum(
        "bhqk,bkhd->bqhd", grad_s_b, rows_of(key_b, groups), preferred_element_type=jnp.float32
    )
    grad_k = jnp.einsum(
        "bhqk,bqhd->bkhd", grad_s_b, rows_of(query_b, groups), preferred_element_type=jnp.float32
    )
    return jnp.concatenate(
        [grad_q.reshape(-1, D), grad_k.reshape(-1, D), grad_v.reshape(-1, D)], axis=1
    )


def layer_forward(x_in, visible, params):
    w_qkv, w_out, w_up, w_down, vec = params
    bias_q, bias_v, bias_o, gain1, shift1, bias_up, bias_down, gain2, shift2 = split_vector(vec)
    projected = jnp.dot(x_in, w_qkv, preferred_element_type=jnp.float32)
    query_b = (projected[:, :D] + bias_q).astype(jnp.bfloat16)
    key_b = projected[:, D : 2 * D].astype(jnp.bfloat16)
    value_b = (projected[:, 2 * D :] + bias_v).astype(jnp.bfloat16)
    log_total, context = attend(query_b, key_b, value_b, visible)
    pre_one = (
        x_in.astype(jnp.float32)
        + jnp.dot(context.astype(jnp.bfloat16), w_out, preferred_element_type=jnp.float32)
        + bias_o
    )
    normed1, inv_std1 = normalize(pre_one)
    hidden1 = normed1 * gain1 + shift1
    hidden1_b = hidden1.astype(jnp.bfloat16)
    up_pre = jnp.dot(hidden1_b, w_up, preferred_element_type=jnp.float32) + bias_up
    act_b = gelu_value(up_pre).astype(jnp.bfloat16)
    pre_two = hidden1 + jnp.dot(act_b, w_down, preferred_element_type=jnp.float32) + bias_down
    normed2, inv_std2 = normalize(pre_two)
    result = normed2 * gain2 + shift2
    kept_state = (
        x_in,
        query_b,
        key_b,
        value_b,
        log_total,
        context,
        normed1,
        inv_std1,
        hidden1_b,
        up_pre,
        act_b,
        normed2,
        inv_std2,
    )
    return (result, kept_state)


def layer_backward(d_out, kept_state, visible, params):
    w_qkv, w_out, w_up, w_down, vec = params
    bias_q, bias_v, bias_o, gain1, shift1, bias_up, bias_down, gain2, shift2 = split_vector(vec)
    (
        x_in,
        query_b,
        key_b,
        value_b,
        log_total,
        context,
        normed1,
        inv_std1,
        hidden1_b,
        up_pre,
        act_b,
        normed2,
        inv_std2,
    ) = kept_state
    grad_gain2 = jnp.sum(d_out * normed2, axis=0)
    grad_shift2 = jnp.sum(d_out, axis=0)
    grad_pre2 = norm_back(d_out * gain2, normed2, inv_std2)
    grad_pre2_b = grad_pre2.astype(jnp.bfloat16)
    grad_bdown = jnp.sum(grad_pre2, axis=0)
    grad_up = right_dot(grad_pre2_b, w_down) * gelu_slope(up_pre)
    grad_up_b = grad_up.astype(jnp.bfloat16)
    grad_bup = jnp.sum(grad_up, axis=0)
    grad_h1 = grad_pre2 + right_dot(grad_up_b, w_up)
    grad_gain1 = jnp.sum(grad_h1 * normed1, axis=0)
    grad_shift1 = jnp.sum(grad_h1, axis=0)
    grad_pre1 = norm_back(grad_h1 * gain1, normed1, inv_std1)
    grad_pre1_b = grad_pre1.astype(jnp.bfloat16)
    grad_bout = jnp.sum(grad_pre1, axis=0)
    context_b = context.astype(jnp.bfloat16)
    grad_ctx_b = right_dot(grad_pre1_b, w_out).astype(jnp.bfloat16)
    grad_proj = attend_back(grad_ctx_b, query_b, key_b, value_b, log_total, context, visible)
    grad_proj_b = grad_proj.astype(jnp.bfloat16)
    grad_bq = jnp.sum(grad_proj[:, :D], axis=0)
    grad_bv = jnp.sum(grad_proj[:, 2 * D :], axis=0)
    grad_x = grad_pre1 + right_dot(grad_proj_b, w_qkv)
    grad_vec = jnp.concatenate(
        [
            grad_bq,
            grad_bv,
            grad_bout,
            grad_gain1,
            grad_shift1,
            grad_bup,
            grad_bdown,
            grad_gain2,
            grad_shift2,
        ]
    )
    operands = (
        (x_in, grad_proj_b),
        (context_b, grad_pre1_b),
        (hidden1_b, grad_up_b),
        (act_b, grad_pre2_b),
    )
    return (grad_x, grad_vec, operands)


def column_blocks(matrix):
    return [matrix[:, start : start + D] for start in range(0, matrix.shape[1], D)]


def pack_shards(w_qkv, w_out, w_up, w_down, vec):
    padded = jnp.pad(vec[None, :], ((0, 15), (0, D - vec.shape[0])))
    blocks = [*column_blocks(w_qkv), *column_blocks(w_up), w_out, w_down, padded]
    return jnp.concatenate(blocks, axis=0)


def unpack_params(packed, rows, down_rows, share):
    count = packed.shape[0]

    def block(index, height=rows):
        return packed[:, index * rows : index * rows + height].reshape(count * height, D)

    full_qkv = jnp.concatenate([block(index) for index in range(3)], axis=1)
    full_up = jnp.concatenate([block(index) for index in range(3, 7)], axis=1)
    vec = packed[:, 8 * rows + down_rows, :share].reshape(-1)
    return full_qkv, block(7), full_up, block(8, down_rows), vec


def gather_params(shards):
    packed = lax.all_gather(pack_shards(*shards), "fsdp", axis=0)
    return unpack_params(packed, shards[1].shape[0], shards[3].shape[0], shards[4].shape[0])


def scatter_grads(operands, vec_grad):
    count = lax.axis_size("fsdp")
    qkv_pair, out_pair, up_pair, down_pair = operands
    share = vec_grad.shape[0] // count
    rows = D // count
    blocks = [left_dot(qkv_pair[0], block) for block in column_blocks(qkv_pair[1])]
    blocks += [left_dot(up_pair[0], block) for block in column_blocks(up_pair[1])]
    blocks += [left_dot(*out_pair), left_dot(*down_pair)]
    blocks = [block.astype(jnp.bfloat16).reshape(count, -1, D) for block in blocks]
    vec_block = vec_grad.astype(jnp.bfloat16).reshape(count, 1, share)
    blocks.append(jnp.pad(vec_block, ((0, 0), (0, 15), (0, D - share))))
    packed = jnp.concatenate(blocks, axis=1)
    total = lax.psum_scatter(packed, "fsdp", scatter_dimension=0).astype(jnp.float32)
    pieces = [total[index * rows : (index + 1) * rows] for index in range(8)]
    last = total.shape[0] - 16
    return (
        jnp.concatenate(pieces[:3], axis=1),
        pieces[7],
        jnp.concatenate(pieces[3:7], axis=1),
        total[8 * rows : last],
        total[last, :share],
    )


def body(ends, lengths, w_qkv, w_out, w_up, w_down, vectors):
    is_first = lax.axis_index("section") == 0
    micro, row_count = ends.shape[1], ends.shape[3]
    local_rows = ends[0, :, 0].reshape(micro * row_count, D)
    positions = jnp.arange(row_count, dtype=jnp.int32)
    visible = positions[None, :] < lengths[:, 0][:, None]
    params = gather_params((w_qkv[0], w_out[0], w_up[0], w_down[0], vectors[0]))
    early, _ = layer_forward(local_rows, visible, params)
    received = shifted(early.astype(jnp.bfloat16), "section", 1)
    x_in = jnp.where(is_first, local_rows, received)
    result, kept_state = layer_forward(x_in, visible, params)
    row_mask = visible.reshape(-1, 1).astype(jnp.float32)
    cotangent = local_rows.astype(jnp.float32) * row_mask
    early_grad, _, _ = layer_backward(cotangent, kept_state, visible, params)
    back_received = shifted(early_grad.astype(jnp.bfloat16), "section", -1)
    d_out = jnp.where(is_first, back_received.astype(jnp.float32), cotangent)
    grad_x, grad_vec, operands = layer_backward(d_out, kept_state, visible, params)
    grad_qkv, grad_out, grad_up, grad_down, grad_vectors = scatter_grads(operands, grad_vec)
    ends_out = jnp.where(is_first, grad_x, result).reshape(1, micro, 1, row_count, D)
    return (
        ends_out,
        grad_qkv[None],
        grad_out[None],
        grad_up[None],
        grad_down[None],
        grad_vectors[None],
    )


def solution(mesh):
    in_specs = (
        P("section", None, "fsdp", None, None),
        P(None, "fsdp"),
        P("section", "fsdp", None),
        P("section", "fsdp", None),
        P("section", "fsdp", None),
        P("section", "fsdp", None),
        P("section", "fsdp"),
    )
    out_specs = (
        P("section", None, "fsdp", None, None),
        P("section", "fsdp", None),
        P("section", "fsdp", None),
        P("section", "fsdp", None),
        P("section", "fsdp", None),
        P("section", "fsdp"),
    )
    return jax.shard_map(body, mesh=mesh, in_specs=in_specs, out_specs=out_specs, check_vma=False)
```

```python
import jax
import jax.numpy as jnp
from jax import lax
from jax.sharding import PartitionSpec as P

D = 768
HEADS = 12
FF = 3072
HEAD = 64


def shifted(value, axis, steps):
    count = lax.axis_size(axis)
    first, last = (max(0, -steps), min(count, count - steps))
    return lax.ppermute(value, axis, [(source, source + steps) for source in range(first, last)])


def split_vector(vec):
    flat_vec = vec.astype(jnp.float32)
    widths = [D, D, D, D, D, FF, D, D, D]
    pieces = []
    offset = 0
    for width in widths:
        pieces.append(flat_vec[offset : offset + width])
        offset = offset + width
    return tuple(pieces)


def normalize(hidden):
    mean_row = jnp.mean(hidden, axis=-1, keepdims=True)
    centred = hidden - mean_row
    variance = jnp.mean(centred * centred, axis=-1, keepdims=True)
    inv_std = lax.rsqrt(variance + 1e-12)
    return (centred * inv_std, inv_std)


def norm_back(grad_n, normed, inv_std):
    return inv_std * (
        grad_n
        - jnp.mean(grad_n, axis=-1, keepdims=True)
        - normed * jnp.mean(grad_n * normed, axis=-1, keepdims=True)
    )


def gelu_value(up_in):
    return 0.5 * up_in * (1.0 + lax.erf(up_in * 0.7071067811865476))


def gelu_slope(up_in):
    return (
        0.5 * (1.0 + lax.erf(up_in * 0.7071067811865476))
        + up_in * jnp.exp(-0.5 * up_in * up_in) * 0.3989422804014327
    )


def left_dot(left, right):
    return lax.dot_general(
        left, right, (((0,), (0,)), ((), ())), preferred_element_type=jnp.float32
    )


def right_dot(left, right):
    return lax.dot_general(
        left, right, (((1,), (1,)), ((), ())), preferred_element_type=jnp.float32
    )


def rows_of(value, groups):
    return value.reshape(groups, value.shape[0] // groups, HEADS, HEAD)


def scores_of(query_b, key_b, visible):
    groups = visible.shape[0]
    scores = jnp.einsum(
        "bqhd,bkhd->bhqk",
        rows_of(query_b, groups),
        rows_of(key_b, groups),
        preferred_element_type=jnp.float32,
    ) * HEAD ** (-0.5)
    return jnp.where(visible[:, None, None, :], scores, -1e30)


def attend(query_b, key_b, value_b, visible):
    groups = visible.shape[0]
    masked = scores_of(query_b, key_b, visible)
    row_peak = jnp.max(masked, axis=-1, keepdims=True)
    log_total = row_peak + jnp.log(jnp.sum(jnp.exp(masked - row_peak), axis=-1, keepdims=True))
    probs_b = jnp.exp(masked - log_total).astype(jnp.bfloat16)
    context = jnp.einsum(
        "bhqk,bkhd->bqhd", probs_b, rows_of(value_b, groups), preferred_element_type=jnp.float32
    )
    return (log_total, context.reshape(-1, D))


def attend_back(grad_ctx_b, query_b, key_b, value_b, log_total, context, visible):
    groups = visible.shape[0]
    masked = scores_of(query_b, key_b, visible)
    attn_probs = jnp.exp(masked - log_total)
    probs_b = attn_probs.astype(jnp.bfloat16)
    grad_heads = rows_of(grad_ctx_b, groups)
    grad_v = jnp.einsum("bhqk,bqhd->bkhd", probs_b, grad_heads, preferred_element_type=jnp.float32)
    grad_p = jnp.einsum(
        "bqhd,bkhd->bhqk", grad_heads, rows_of(value_b, groups), preferred_element_type=jnp.float32
    )
    delta_rows = jnp.sum(grad_heads.astype(jnp.float32) * rows_of(context, groups), axis=-1)
    grad_s = attn_probs * (grad_p - jnp.swapaxes(delta_rows, 1, 2)[..., None]) * HEAD ** (-0.5)
    grad_s_b = grad_s.astype(jnp.bfloat16)
    grad_q = jnp.einsum(
        "bhqk,bkhd->bqhd", grad_s_b, rows_of(key_b, groups), preferred_element_type=jnp.float32
    )
    grad_k = jnp.einsum(
        "bhqk,bqhd->bkhd", grad_s_b, rows_of(query_b, groups), preferred_element_type=jnp.float32
    )
    return jnp.concatenate(
        [grad_q.reshape(-1, D), grad_k.reshape(-1, D), grad_v.reshape(-1, D)], axis=1
    )


def layer_forward(x_in, visible, params):
    w_qkv, w_out, w_up, w_down, vec = params
    bias_q, bias_v, bias_o, gain1, shift1, bias_up, bias_down, gain2, shift2 = split_vector(vec)
    projected = jnp.dot(x_in, w_qkv, preferred_element_type=jnp.float32)
    query_b = (projected[:, :D] + bias_q).astype(jnp.bfloat16)
    key_b = projected[:, D : 2 * D].astype(jnp.bfloat16)
    value_b = (projected[:, 2 * D :] + bias_v).astype(jnp.bfloat16)
    log_total, context = attend(query_b, key_b, value_b, visible)
    pre_one = (
        x_in.astype(jnp.float32)
        + jnp.dot(context.astype(jnp.bfloat16), w_out, preferred_element_type=jnp.float32)
        + bias_o
    )
    normed1, inv_std1 = normalize(pre_one)
    hidden1 = normed1 * gain1 + shift1
    hidden1_b = hidden1.astype(jnp.bfloat16)
    up_pre = jnp.dot(hidden1_b, w_up, preferred_element_type=jnp.float32) + bias_up
    act_b = gelu_value(up_pre).astype(jnp.bfloat16)
    pre_two = hidden1 + jnp.dot(act_b, w_down, preferred_element_type=jnp.float32) + bias_down
    normed2, inv_std2 = normalize(pre_two)
    result = normed2 * gain2 + shift2
    kept_state = (
        x_in,
        query_b,
        key_b,
        value_b,
        log_total,
        context,
        normed1,
        inv_std1,
        hidden1_b,
        up_pre,
        act_b,
        normed2,
        inv_std2,
    )
    return (result, kept_state)


def layer_backward(d_out, kept_state, visible, params):
    w_qkv, w_out, w_up, w_down, vec = params
    bias_q, bias_v, bias_o, gain1, shift1, bias_up, bias_down, gain2, shift2 = split_vector(vec)
    (
        x_in,
        query_b,
        key_b,
        value_b,
        log_total,
        context,
        normed1,
        inv_std1,
        hidden1_b,
        up_pre,
        act_b,
        normed2,
        inv_std2,
    ) = kept_state
    grad_gain2 = jnp.sum(d_out * normed2, axis=0)
    grad_shift2 = jnp.sum(d_out, axis=0)
    grad_pre2 = norm_back(d_out * gain2, normed2, inv_std2)
    grad_pre2_b = grad_pre2.astype(jnp.bfloat16)
    grad_bdown = jnp.sum(grad_pre2, axis=0)
    grad_up = right_dot(grad_pre2_b, w_down) * gelu_slope(up_pre)
    grad_up_b = grad_up.astype(jnp.bfloat16)
    grad_bup = jnp.sum(grad_up, axis=0)
    grad_h1 = grad_pre2 + right_dot(grad_up_b, w_up)
    grad_gain1 = jnp.sum(grad_h1 * normed1, axis=0)
    grad_shift1 = jnp.sum(grad_h1, axis=0)
    grad_pre1 = norm_back(grad_h1 * gain1, normed1, inv_std1)
    grad_pre1_b = grad_pre1.astype(jnp.bfloat16)
    grad_bout = jnp.sum(grad_pre1, axis=0)
    context_b = context.astype(jnp.bfloat16)
    grad_ctx_b = right_dot(grad_pre1_b, w_out).astype(jnp.bfloat16)
    grad_proj = attend_back(grad_ctx_b, query_b, key_b, value_b, log_total, context, visible)
    grad_proj_b = grad_proj.astype(jnp.bfloat16)
    grad_bq = jnp.sum(grad_proj[:, :D], axis=0)
    grad_bv = jnp.sum(grad_proj[:, 2 * D :], axis=0)
    grad_x = grad_pre1 + right_dot(grad_proj_b, w_qkv)
    grad_vec = jnp.concatenate(
        [
            grad_bq,
            grad_bv,
            grad_bout,
            grad_gain1,
            grad_shift1,
            grad_bup,
            grad_bdown,
            grad_gain2,
            grad_shift2,
        ]
    )
    operands = (
        (x_in, grad_proj_b),
        (context_b, grad_pre1_b),
        (hidden1_b, grad_up_b),
        (act_b, grad_pre2_b),
    )
    return (grad_x, grad_vec, operands)


def column_blocks(matrix):
    return [matrix[:, start : start + D] for start in range(0, matrix.shape[1], D)]


def pack_shards(w_qkv, w_out, w_up, w_down, vec):
    padded = jnp.pad(vec[None, :], ((0, 15), (0, D - vec.shape[0])))
    blocks = [*column_blocks(w_qkv), *column_blocks(w_up), w_out, w_down, padded]
    return jnp.concatenate(blocks, axis=0)


def unpack_params(packed, rows, down_rows, share):
    count = packed.shape[0]

    def block(index, height=rows):
        return packed[:, index * rows : index * rows + height].reshape(count * height, D)

    full_qkv = jnp.concatenate([block(index) for index in range(3)], axis=1)
    full_up = jnp.concatenate([block(index) for index in range(3, 7)], axis=1)
    vec = packed[:, 8 * rows + down_rows, :share].reshape(-1)
    return full_qkv, block(7), full_up, block(8, down_rows), vec


def gather_params(shards):
    packed = lax.all_gather(pack_shards(*shards), "fsdp", axis=0)
    return unpack_params(packed, shards[1].shape[0], shards[3].shape[0], shards[4].shape[0])


def scatter_blocks(blocks):
    count = lax.axis_size("fsdp")
    blocks = [block.astype(jnp.bfloat16).reshape(count, -1, block.shape[-1]) for block in blocks]
    packed = jnp.concatenate(blocks, axis=1)
    return lax.psum_scatter(packed, "fsdp", scatter_dimension=0).astype(jnp.float32)


def joined_columns(total, rows, blocks):
    pieces = [total[index * rows : (index + 1) * rows] for index in range(blocks)]
    return jnp.concatenate(pieces, axis=1)


def scatter_grads(operands, vec_grad):
    count = lax.axis_size("fsdp")
    qkv_pair, out_pair, up_pair, down_pair = operands
    share = vec_grad.shape[0] // count
    rows = D // count
    up_blocks = [left_dot(up_pair[0], block) for block in column_blocks(up_pair[1])]
    mlp_total = scatter_blocks([*up_blocks, left_dot(*down_pair)])
    blocks = [left_dot(qkv_pair[0], block) for block in column_blocks(qkv_pair[1])]
    vec_block = jnp.pad(vec_grad.reshape(count, 1, share), ((0, 0), (0, 15), (0, D - share)))
    rest = scatter_blocks([*blocks, left_dot(*out_pair), vec_block])
    return (
        joined_columns(rest, rows, 3),
        rest[3 * rows : 4 * rows],
        joined_columns(mlp_total, rows, 4),
        mlp_total[4 * rows :],
        rest[4 * rows, :share],
    )


def body(ends, lengths, w_qkv, w_out, w_up, w_down, vectors):
    is_first = lax.axis_index("section") == 0
    micro, row_count = ends.shape[1], ends.shape[3]
    local_rows = ends[0, :, 0].reshape(micro * row_count, D)
    positions = jnp.arange(row_count, dtype=jnp.int32)
    visible = positions[None, :] < lengths[:, 0][:, None]
    params = gather_params((w_qkv[0], w_out[0], w_up[0], w_down[0], vectors[0]))
    early, _ = layer_forward(local_rows, visible, params)
    received = shifted(early.astype(jnp.bfloat16), "section", 1)
    x_in = jnp.where(is_first, local_rows, received)
    result, kept_state = layer_forward(x_in, visible, params)
    row_mask = visible.reshape(-1, 1).astype(jnp.float32)
    cotangent = local_rows.astype(jnp.float32) * row_mask
    early_grad, _, _ = layer_backward(cotangent, kept_state, visible, params)
    back_received = shifted(early_grad.astype(jnp.bfloat16), "section", -1)
    d_out = jnp.where(is_first, back_received.astype(jnp.float32), cotangent)
    grad_x, grad_vec, operands = layer_backward(d_out, kept_state, visible, params)
    grad_qkv, grad_out, grad_up, grad_down, grad_vectors = scatter_grads(operands, grad_vec)
    ends_out = jnp.where(is_first, grad_x, result).reshape(1, micro, 1, row_count, D)
    return (
        ends_out,
        grad_qkv[None],
        grad_out[None],
        grad_up[None],
        grad_down[None],
        grad_vectors[None],
    )


def solution(mesh):
    in_specs = (
        P("section", None, "fsdp", None, None),
        P(None, "fsdp"),
        P("section", "fsdp", None),
        P("section", "fsdp", None),
        P("section", "fsdp", None),
        P("section", "fsdp", None),
        P("section", "fsdp"),
    )
    out_specs = (
        P("section", None, "fsdp", None, None),
        P("section", "fsdp", None),
        P("section", "fsdp", None),
        P("section", "fsdp", None),
        P("section", "fsdp", None),
        P("section", "fsdp"),
    )
    return jax.shard_map(body, mesh=mesh, in_specs=in_specs, out_specs=out_specs, check_vma=False)
```
